256 devices in a mesh: node: 32 (over y, x, core), chip: 8 (over z).
Axes of the slice: x: 4, y: 4, z: 8, core: 2. Of those that a mesh axis runs over, the one named last changes fastest.
Arguments:
- activations: bfloat16 [32768, 1984], P(('node', 'chip')), may hold values from -6 to 6
- hidden_grad: bfloat16 [32768, 7936], P(('node', 'chip')), may hold values from -0.5 to 0.5
- feedback: bfloat16 [63488, 7936], P(('node', 'chip')), may hold values from -6 to 6
- q_start: bfloat16 [7936, 128], P('chip'), may hold values from -0.0625 to 0.0625
Outputs:
- new_feedback: bfloat16 [63488, 7936], P(('node', 'chip'))
- p_hat: float32 [1984, 128], P('chip')
- q_new: float32 [7936, 128], P('chip')
The draws below stay inside these ranges and needn't reach their ends.
All inputs are finite; a program needn't handle non-finite values.
Results may differ from the reference program's by a relative error of at most 0.012.
Values may be sent and summed in bfloat16 or wider, within the bound.
A program may use at most 192 MiB of HBM per device.

```python
import jax
import jax.numpy as jnp
from jax import lax

R = 1984
C = 7936
RANK = 128
TOK_DEV = 128
TOKENS = 32768
N_NODE = 32
N_CHIP = 8


def steps_of(rng, extent, shards, low, top_value):
    gain, own = 1.0, jax.random.fold_in(rng, 6)
    for dim, blocks in shards:
        draws = jnp.exp(jax.random.uniform(jax.random.fold_in(own, dim), (blocks,), jnp.float32, low / len(shards), top_value / len(shards)))
        gain = gain * jnp.repeat(draws, extent[dim] // blocks).reshape([-1 if axis == dim else 1 for axis in range(len(extent))])
    return gain


def scatter_about(stream_key, extent, width, bound, split=(), kind=jnp.bfloat16):
    values = jax.random.normal(stream_key, extent, jnp.float32) * width
    if len(split) > 0:
        values = steps_of(stream_key, extent, split, -0.22, 0.18) * values
    return jnp.clip(values, min=-bound, max=bound).astype(kind)


def setup_inputs(seed: int = 0) -> dict:
    key_list = jax.random.split(jax.random.key(seed), 5)
    activations = scatter_about(key_list[0], (TOKENS, R), 1.0, 6.0, ((0, 256),))
    hidden_grad = scatter_about(key_list[1], (TOKENS, C), ((N_CHIP * TOK_DEV) ** -0.5), 0.5, ((0, 256),))
    feedback = scatter_about(key_list[2], (N_NODE * R, C), 1.0, 6.0, ((0, 256),))
    q_start = scatter_about(key_list[3], (C, RANK), C ** -0.5, 0.0625, ((0, 8),))
    return {"activations": activations, "hidden_grad": hidden_grad, "feedback": feedback, "q_start": q_start}


def reference(activations, hidden_grad, feedback, q_start):
    per_node = TOK_DEV * N_CHIP
    acts = activations.reshape(N_NODE, per_node, R)
    grads = hidden_grad.reshape(N_NODE, per_node, C)
    carried = feedback.reshape(N_NODE, R, C)

    def accumulate(items):
        left, right, error_part = items
        summed = lax.dot_general(left.astype(jnp.float32), right.astype(jnp.float32), (((0,), (0,)), ((), ())), preferred_element_type=jnp.float32)
        return summed + error_part.astype(jnp.float32)
    accum = lax.map(accumulate, (acts, grads, carried))
    accum_low = accum.astype(jnp.bfloat16)
    p_parts = lax.map(lambda matrix: jnp.dot(matrix.astype(jnp.float32), q_start.astype(jnp.float32), preferred_element_type=jnp.float32), accum_low)
    p_total = jnp.sum(p_parts, axis=0)
    gram = jnp.dot(p_total.T, p_total, precision=lax.Precision.HIGHEST)
    factor = jnp.linalg.cholesky(gram)
    p_hat = jax.scipy.linalg.solve_triangular(factor, p_total.T, lower=True).T
    p_hat_low = p_hat.astype(jnp.bfloat16)
    q_parts = lax.map(lambda matrix: lax.dot_general(matrix.astype(jnp.float32), p_hat_low.astype(jnp.float32), (((0,), (0,)), ((), ())), preferred_element_type=jnp.float32), accum_low)
    q_new = jnp.sum(q_parts, axis=0) / N_NODE
    q_low = q_new.astype(jnp.bfloat16)
    update = lax.dot_general(p_hat_low.astype(jnp.float32), q_low.astype(jnp.float32), (((1,), (1,)), ((), ())), preferred_element_type=jnp.float32)
    new_feedback = (accum - update[None]).astype(jnp.bfloat16).reshape(N_NODE * R, C)
    return (new_feedback, p_hat, q_new)
```

```python
import functools

import jax
import jax.numpy as jnp
from jax import lax
from jax.experimental import pallas as pl
from jax.experimental.pallas import tpu as pltpu
from jax.sharding import PartitionSpec as P

MESH = pl.DeviceIdType.MESH
F32, BF16 = jnp.float32, jnp.bfloat16
CHIPS, SIDE, CORES = 8, 4, 2
ROWS, COLS, RANK, TOK = 248, 7936, 128, 128
PAD_ROWS = 256
LANES = 256
BLOCKS = COLS // LANES


class Place:
    def __init__(self):
        node = lax.axis_index("node")
        self.core = lax.rem(node, CORES)
        self.x = lax.rem(lax.div(node, CORES), SIDE)
        self.y = lax.div(node, CORES * SIDE)
        self.z = lax.axis_index("chip")

    def node(self, y, x, core):
        return (y * SIDE + x) * CORES + core

    def axis(self, name):
        if name == "z":
            return CHIPS, self.z, lambda j: {"chip": j}
        if name == "y":
            return SIDE, self.y, lambda j: {"node": self.node(j, self.x, self.core)}
        if name == "x":
            return SIDE, self.x, lambda j: {"node": self.node(self.y, j, self.core)}
        return CORES, self.core, lambda j: {"node": self.node(self.y, self.x, j)}


def barrier(place):
    sem = pltpu.get_barrier_semaphore()
    count = 0
    for name in ("z", "y", "x", "core"):
        size, own, device = place.axis(name)
        for step in range(1, size):
            pl.semaphore_signal(
                sem, inc=1, device_id=device(lax.rem(own + step, size)), device_id_type=MESH
            )
            count += 1
    pl.semaphore_wait(sem, count)


class Sems:
    def __init__(self, send, recv):
        self.send, self.recv, self.used = send, recv, 0

    def take(self):
        self.used += 1
        return self.send.at[self.used - 1], self.recv.at[self.used - 1]


class Exchange:
    def __init__(self, place, name, sems, source, landing):
        size, own, device = place.axis(name)
        self.copies = []
        for step in range(1, size):
            to, of = lax.rem(own + step, size), lax.rem(own + size - step, size)
            send, recv = sems.take()
            self.copies.append(
                (
                    pltpu.make_async_remote_copy(
                        src_ref=source(to),
                        dst_ref=landing(step, own),
                        send_sem=send,
                        recv_sem=recv,
                        device_id=device(to),
                        device_id_type=MESH,
                    ),
                    pltpu.make_async_remote_copy(
                        src_ref=landing(step, of),
                        dst_ref=landing(step, of),
                        send_sem=send,
                        recv_sem=recv,
                        device_id=device(to),
                        device_id_type=MESH,
                    ),
                )
            )
        for out, _ in self.copies:
            out.start()

    def arrive(self):
        for _, inward in self.copies:
            inward.wait_recv()

    def sent(self):
        for out, _ in self.copies:
            out.wait_send()


def gather_over(place, name, sems, slot):
    own = place.axis(name)[1]
    return Exchange(place, name, sems, lambda j: slot(own), lambda step, j: slot(j))


def scatter_over(place, name, sems, parts, received):
    return Exchange(
        place, name, sems, lambda j: parts.at[j], lambda step, j: received.at[step - 1]
    )


def left_kernel(
    at_ref, g_hbm, f_hbm, q_ref, p_ref, ar_ref,
    g_ref, f_ref, qb, qs, tb, fq, pp, p_core, p_one, p_x, p_two, p_y,
    load_sem, send_sem, recv_sem,
):
    place = Place()
    core, x, y, z = place.core, place.x, place.y, place.z
    sems = Sems(send_sem, recv_sem)
    load_g = pltpu.make_async_copy(g_hbm, g_ref, load_sem.at[0])
    load_f = pltpu.make_async_copy(f_hbm, f_ref, load_sem.at[1])
    load_g.start()
    load_f.start()
    own_acts = pltpu.make_async_copy(at_ref.at[z], ar_ref.at[z], load_sem.at[2])
    own_acts.start()
    part = (core * SIDE + x) * SIDE + y
    own_q = pltpu.make_async_copy(q_ref.at[part], qb.at[core, x, y, z], load_sem.at[3])
    own_q.start()
    own_q.wait()
    barrier(place)

    done = []
    step = gather_over(place, "z", sems, lambda j: qb.at[core, x, y, j])
    acts = Exchange(place, "z", sems, lambda j: at_ref.at[j], lambda s, j: ar_ref.at[j])
    done += [step, acts]
    step.arrive()
    for name, slot in (
        ("y", lambda j: qb.at[core, x, j]),
        ("x", lambda j: qb.at[core, j]),
        ("core", lambda j: qb.at[j]),
    ):
        step = gather_over(place, name, sems, slot)
        done.append(step)
        step.arrive()

    def place_rows(i, carry):
        for c in range(CHIPS):
            qs[pl.ds(pl.multiple_of(c * 992 + i * 32, 32), 32), :] = qb[
                lax.div(i, 16), lax.rem(lax.div(i, 4), 4), lax.rem(i, 4), c
            ]
        return carry

    lax.fori_loop(0, 31, place_rows, 0)

    def times_q(ref, i):
        at = pl.multiple_of(i * LANES, LANES)
        return jnp.dot(
            ref[:, pl.ds(at, LANES)], qs[pl.ds(at, LANES), :], preferred_element_type=F32
        )

    load_g.wait()
    projected = lax.fori_loop(
        0, BLOCKS, lambda i, total: total + times_q(g_ref, i), jnp.zeros((TOK, RANK), F32)
    )
    tb[z] = projected.astype(BF16)
    tokens = gather_over(place, "z", sems, lambda j: tb.at[j])
    done.append(tokens)
    load_f.wait()
    fq[...] = jnp.zeros_like(fq)
    fq[:ROWS, :] = lax.fori_loop(
        0, BLOCKS, lambda i, total: total + times_q(f_ref, i), jnp.zeros((ROWS, RANK), F32)
    )
    own_acts.wait()
    acts.arrive()
    tokens.arrive()
    total = fq[...]
    for b in range(CHIPS):
        total += jnp.dot(ar_ref[b], tb[b], preferred_element_type=F32)
    pp[...] = total.reshape(pp.shape)

    step = scatter_over(place, "core", sems, pp, p_core)
    done.append(step)
    step.arrive()
    p_one[...] = pp[core] + p_core[0]
    step = scatter_over(place, "x", sems, p_one, p_x)
    done.append(step)
    step.arrive()
    p_two[...] = p_one[x] + p_x[0] + p_x[1] + p_x[2]
    step = scatter_over(place, "y", sems, p_two, p_y)
    done.append(step)
    step.arrive()
    p_ref[core, x, y, z] = p_two[y] + p_y[0] + p_y[1] + p_y[2]
    for name, slot in (
        ("z", lambda j: p_ref.at[core, x, y, j]),
        ("y", lambda j: p_ref.at[core, x, j]),
        ("x", lambda j: p_ref.at[core, j]),
        ("core", lambda j: p_ref.at[j]),
    ):
        step = gather_over(place, name, sems, slot)
        done.append(step)
        step.arrive()
    for step in done:
        step.sent()


def left(at, g, f, q):
    copies = (7 + 3 + 3 + 1) * 2 + 7 + 7 + (1 + 3 + 3)
    vmem = pl.BlockSpec(memory_space=pltpu.VMEM)
    hbm = pl.BlockSpec(memory_space=pl.ANY)
    return pl.pallas_call(
        left_kernel,
        out_shape=(
            jax.ShapeDtypeStruct((CORES, SIDE, SIDE, CHIPS, 8, RANK), F32),
            jax.ShapeDtypeStruct((CHIPS, PAD_ROWS, TOK), BF16),
        ),
        in_specs=[vmem, hbm, hbm, vmem],
        out_specs=(vmem, vmem),
        scratch_shapes=[
            pltpu.VMEM((TOK, COLS), BF16),
            pltpu.VMEM((ROWS, COLS), BF16),
            pltpu.VMEM((CORES, SIDE, SIDE, CHIPS, 32, RANK), BF16),
            pltpu.VMEM((COLS, RANK), BF16),
            pltpu.VMEM((CHIPS, TOK, RANK), BF16),
            pltpu.VMEM((PAD_ROWS, RANK), F32),
            pltpu.VMEM((CORES, SIDE, SIDE, 8, RANK), F32),
            pltpu.VMEM((1, SIDE, SIDE, 8, RANK), F32),
            pltpu.VMEM((SIDE, SIDE, 8, RANK), F32),
            pltpu.VMEM((3, SIDE, 8, RANK), F32),
            pltpu.VMEM((SIDE, 8, RANK), F32),
            pltpu.VMEM((3, 8, RANK), F32),
            pltpu.SemaphoreType.DMA((4,)),
            pltpu.SemaphoreType.DMA((copies,)),
            pltpu.SemaphoreType.DMA((copies,)),
        ],
        compiler_params=pltpu.CompilerParams(
            collective_id=0, has_side_effects=True, vmem_limit_bytes=32 * 2**20
        ),
        cost_estimate=pl.CostEstimate(flops=10**9, bytes_accessed=150 * 10**6, transcendentals=0),
    )(at, g, f, q)


def right_kernel(
    at_ref, p_ref, g_hbm, f_hbm, q_ref,
    g_ref, f_ref, w, w_core, w_one, w_x, w_two, w_y, w_three, w_z,
    load_sem, send_sem, recv_sem,
):
    place = Place()
    core, x, y, z = place.core, place.x, place.y, place.z
    sems = Sems(send_sem, recv_sem)
    load_g = pltpu.make_async_copy(g_hbm, g_ref, load_sem.at[0])
    load_f = pltpu.make_async_copy(f_hbm, f_ref, load_sem.at[1])
    load_g.start()
    load_f.start()
    barrier(place)

    u = jnp.zeros((RANK, TOK), F32)
    for c in range(CHIPS):
        u += lax.dot_general(
            p_ref[c], at_ref[c], (((0,), (0,)), ((), ())), preferred_element_type=F32
        )
    u = u.astype(BF16)
    own_p = p_ref[z].T[:, :ROWS]
    load_g.wait()
    load_f.wait()

    def fill(i, carry):
        at = pl.multiple_of(i * LANES, LANES)
        term = jnp.dot(u, g_ref[:, pl.ds(at, LANES)], preferred_element_type=F32)
        term += jnp.dot(own_p, f_ref[:, pl.ds(at, LANES)], preferred_element_type=F32)
        term = term.astype(BF16)
        where = (lax.div(i, 16), lax.rem(lax.div(i, 4), 4), lax.rem(i, 4))
        for k in range(2):
            w[(*where, k)] = term[:, k * 128 : (k + 1) * 128].reshape(CHIPS, 16, 128)
        return carry

    w[CORES - 1, SIDE - 1, SIDE - 1] = jnp.zeros(w.shape[3:], BF16)
    lax.fori_loop(0, BLOCKS, fill, 0)

    done = []
    step = scatter_over(place, "core", sems, w, w_core)
    done.append(step)
    step.arrive()

    def add_core(i, carry):
        w_one[i] = (w[core, i].astype(F32) + w_core[0, i].astype(F32)).astype(BF16)
        return carry

    lax.fori_loop(0, SIDE, add_core, 0)
    step = scatter_over(place, "x", sems, w_one, w_x)
    done.append(step)
    step.arrive()

    def add_x(i, carry):
        w_two[i] = (
            (w_one[x, i].astype(F32) + w_x[0, i].astype(F32))
            + (w_x[1, i].astype(F32) + w_x[2, i].astype(F32))
        ).astype(BF16)
        return carry

    lax.fori_loop(0, SIDE, add_x, 0)
    step = scatter_over(place, "y", sems, w_two, w_y)
    done.append(step)
    step.arrive()
    total = (
        w_two[y].astype(F32) + w_y[0].astype(F32) + w_y[1].astype(F32) + w_y[2].astype(F32)
    ).astype(BF16)
    for c in range(CHIPS):
        w_three[c] = total[:, c]
    step = scatter_over(place, "z", sems, w_three, w_z)
    done.append(step)
    step.arrive()
    mine = w_three[z].astype(F32)
    for c in range(CHIPS - 1):
        mine += w_z[c].astype(F32)
    q_ref[core, x, y, :, z] = (mine * (1.0 / 32)).astype(BF16)
    for name, slot in (
        ("z", lambda j: q_ref.at[core, x, y, :, j]),
        ("y", lambda j: q_ref.at[core, x, j]),
        ("x", lambda j: q_ref.at[core, j]),
        ("core", lambda j: q_ref.at[j]),
    ):
        step = gather_over(place, name, sems, slot)
        done.append(step)
        step.arrive()
    for step in done:
        step.sent()


def right(at, p_low, g, f):
    copies = (7 + 3 + 3 + 1) * 2
    vmem = pl.BlockSpec(memory_space=pltpu.VMEM)
    hbm = pl.BlockSpec(memory_space=pl.ANY)
    return pl.pallas_call(
        right_kernel,
        out_shape=jax.ShapeDtypeStruct((CORES, SIDE, SIDE, 2, CHIPS, 16, 128), BF16),
        in_specs=[vmem, vmem, hbm, hbm],
        out_specs=vmem,
        scratch_shapes=[
            pltpu.VMEM((TOK, COLS), BF16),
            pltpu.VMEM((ROWS, COLS), BF16),
            pltpu.VMEM((CORES, SIDE, SIDE, 2, CHIPS, 16, 128), BF16),
            pltpu.VMEM((1, SIDE, SIDE, 2, CHIPS, 16, 128), BF16),
            pltpu.VMEM((SIDE, SIDE, 2, CHIPS, 16, 128), BF16),
            pltpu.VMEM((3, SIDE, 2, CHIPS, 16, 128), BF16),
            pltpu.VMEM((SIDE, 2, CHIPS, 16, 128), BF16),
            pltpu.VMEM((3, 2, CHIPS, 16, 128), BF16),
            pltpu.VMEM((CHIPS, 2, 16, 128), BF16),
            pltpu.VMEM((CHIPS - 1, 2, 16, 128), BF16),
            pltpu.SemaphoreType.DMA((2,)),
            pltpu.SemaphoreType.DMA((copies,)),
            pltpu.SemaphoreType.DMA((copies,)),
        ],
        compiler_params=pltpu.CompilerParams(
            collective_id=1, has_side_effects=True, vmem_limit_bytes=32 * 2**20
        ),
        cost_estimate=pl.CostEstimate(flops=10**9, bytes_accessed=150 * 10**6, transcendentals=0),
    )(at, p_low, g, f)


def feedback_kernel(ar_ref, g_ref, f_ref, p_ref, q_ref, out_ref):
    grads = g_ref[...].reshape(CHIPS * TOK, LANES)
    total = jnp.dot(ar_ref[...], grads, preferred_element_type=F32)
    for k in range(2):
        at = slice(k * 128, (k + 1) * 128)
        factor = q_ref[k].reshape(RANK, 128)
        update = jnp.dot(p_ref[...], factor, preferred_element_type=F32)
        out_ref[:, at] = (
            (total[:ROWS, at] + f_ref[:, at].astype(F32)) - update[:ROWS]
        ).astype(BF16)


def feedback_of(ar, g_all, f, p_own, q_all):
    return pl.pallas_call(
        feedback_kernel,
        grid=(BLOCKS,),
        out_shape=jax.ShapeDtypeStruct((ROWS, COLS), BF16),
        in_specs=[
            pl.BlockSpec((PAD_ROWS, CHIPS * TOK), lambda i: (0, 0)),
            pl.BlockSpec((CHIPS, TOK, LANES), lambda i: (0, 0, i)),
            pl.BlockSpec((ROWS, LANES), lambda i: (0, i)),
            pl.BlockSpec((PAD_ROWS, RANK), lambda i: (0, 0)),
            pl.BlockSpec((2, CHIPS, 16, 128), lambda i: (i, 0, 0, 0)),
        ],
        out_specs=pl.BlockSpec((ROWS, LANES), lambda i: (0, i)),
        compiler_params=pltpu.CompilerParams(vmem_limit_bytes=32 * 2**20),
    )(ar, g_all, f, p_own, q_all)


def local(activations, hidden_grad, feedback, q_start):
    z = lax.axis_index("chip")
    g_all = lax.all_gather(hidden_grad, "chip", axis=0, tiled=False)
    at = jnp.pad(activations.T.reshape(CHIPS, ROWS, TOK), ((0, 0), (0, PAD_ROWS - ROWS), (0, 0)))
    q_parts = jnp.pad(q_start, ((0, 32), (0, 0))).reshape(32, 32, RANK)
    p_parts, ar = left(at, hidden_grad, feedback, q_parts)
    p_every = p_parts.reshape(32, CHIPS, 8, RANK).transpose(1, 0, 2, 3).reshape(CHIPS * PAD_ROWS, RANK)
    gram = jnp.dot(p_every.T, p_every, precision=lax.Precision.HIGHEST)
    factor = jnp.linalg.cholesky(gram)
    p_hat = jax.scipy.linalg.solve_triangular(factor, p_every.T, lower=True).T
    p_hat = p_hat.reshape(CHIPS, PAD_ROWS, RANK)
    p_low = p_hat.astype(BF16)
    q_all = right(at, p_low, hidden_grad, feedback)
    q_rows = q_all.reshape(64, CHIPS * 16, 128).transpose(0, 2, 1).reshape(64 * 128, RANK)
    q_mine = lax.dynamic_slice_in_dim(q_rows, z * 992, 992, 0).astype(F32)
    p_mine = lax.dynamic_index_in_dim(p_hat, z, 0, keepdims=False)[:ROWS]
    p_own = lax.dynamic_index_in_dim(p_low, z, 0, keepdims=False)
    ar_flat = ar.transpose(1, 0, 2).reshape(PAD_ROWS, CHIPS * TOK)
    new_feedback = feedback_of(ar_flat, g_all, feedback, p_own, q_all.reshape(64, CHIPS, 16, 128))
    return (new_feedback, p_mine, q_mine)


def solution(mesh):
    in_specs = (
        P(("node", "chip"), None),
        P(("node", "chip"), None),
        P(("node", "chip"), None),
        P("chip", None),
    )
    out_specs = (P(("node", "chip"), None), P("chip", None), P("chip", None))
    return jax.shard_map(local, mesh=mesh, in_specs=in_specs, out_specs=out_specs, check_vma=False)
```

```python
import jax
import jax.numpy as jnp
from jax import lax
from jax.experimental import pallas as pl
from jax.experimental.pallas import tpu as pltpu
from jax.sharding import PartitionSpec as P

MESH = pl.DeviceIdType.MESH
F32, BF16 = jnp.float32, jnp.bfloat16
CHIPS, SIDE, CORES = 8, 4, 2
ROWS, COLS, RANK, TOK = 248, 7936, 128, 128
PAD_ROWS = 256
WIDE = 1024
VMEM_MIB = 45
TA, TB, TC, TD, TE, TF = 4, 4, 6, 3, 1, 8
PIECES = 8
PIECE = TOK // PIECES


class Place:
    def __init__(self):
        node = lax.axis_index("node")
        self.core = lax.rem(node, CORES)
        self.x = lax.rem(lax.div(node, CORES), SIDE)
        self.y = lax.div(node, CORES * SIDE)
        self.z = lax.axis_index("chip")

    def node(self, y, x, core):
        return (y * SIDE + x) * CORES + core

    def axis(self, name):
        if name == "z":
            return CHIPS, self.z, lambda j: {"chip": j}
        if name == "y":
            return SIDE, self.y, lambda j: {"node": self.node(j, self.x, self.core)}
        if name == "x":
            return SIDE, self.x, lambda j: {"node": self.node(self.y, j, self.core)}
        return CORES, self.core, lambda j: {"node": self.node(self.y, self.x, j)}


def announce(place):
    sem = pltpu.get_barrier_semaphore()
    count = 0
    for name in ("z", "y", "x", "core"):
        size, own, device = place.axis(name)
        for step in range(1, size):
            pl.semaphore_signal(
                sem, inc=1, device_id=device(lax.rem(own + step, size)), device_id_type=MESH
            )
            count += 1
    return sem, count


class Sems:
    def __init__(self, send, recv):
        self.send, self.recv, self.used = send, recv, 0

    def take(self):
        self.used += 1
        return self.send.at[self.used - 1], self.recv.at[self.used - 1]


class Exchange:
    def __init__(self, place, name, sems, source, landing):
        size, own, device = place.axis(name)
        self.copies = []
        for step in range(1, size):
            to, of = lax.rem(own + step, size), lax.rem(own + size - step, size)
            send, recv = sems.take()
            self.copies.append(
                (
                    pltpu.make_async_remote_copy(
                        src_ref=source(to),
                        dst_ref=landing(step, own),
                        send_sem=send,
                        recv_sem=recv,
                        device_id=device(to),
                        device_id_type=MESH,
                    ),
                    pltpu.make_async_remote_copy(
                        src_ref=landing(step, of),
                        dst_ref=landing(step, of),
                        send_sem=send,
                        recv_sem=recv,
                        device_id=device(to),
                        device_id_type=MESH,
                    ),
                )
            )
        for out, _ in self.copies:
            out.start()

    def arrive(self):
        for _, inward in self.copies:
            inward.wait_recv()

    def sent(self):
        for out, _ in self.copies:
            out.wait_send()


def gather_over(place, name, sems, slot):
    own = place.axis(name)[1]
    return Exchange(place, name, sems, lambda j: slot(own), lambda step, j: slot(j))


def scatter_over(place, name, sems, parts, received):
    return Exchange(
        place, name, sems, lambda j: parts.at[j], lambda step, j: received.at[step - 1]
    )


class Ring:
    TURNS = 3 * PIECES + PIECES // 2

    def __init__(self, place, g_ref, send, recv):
        self.z, self.g, self.send, self.recv = place.z, g_ref, send, recv
        self.device = place.axis("z")[2]
        self.started = self.arrived = 0

    def block(self, way, hops):
        return lax.rem(self.z + (CHIPS - hops if way == 0 else hops), CHIPS)

    def copy(self, way, turn, received):
        hop, i = turn // PIECES + 1, turn % PIECES
        piece = i if way == 0 else PIECES - 1 - i
        view = self.g.at[self.block(way, hop if received else hop - 1), pl.ds(piece * PIECE, PIECE)]
        to = lax.rem(self.z + (1 if way == 0 else CHIPS - 1), CHIPS)
        return pltpu.make_async_remote_copy(
            src_ref=view,
            dst_ref=view,
            send_sem=self.send.at[way, turn],
            recv_sem=self.recv.at[way, turn],
            device_id=self.device(to),
            device_id_type=MESH,
        )

    def arrive(self, turns):
        while self.arrived < turns:
            for way in range(2):
                self.copy(way, self.arrived, True).wait_recv()
            self.arrived += 1

    def pump(self, turns):
        for _ in range(turns):
            self.arrive(self.started + 1 - PIECES)
            for way in range(2):
                self.copy(way, self.started, False).start()
            self.started += 1

    def sent(self):
        for turn in range(self.TURNS):
            for way in range(2):
                self.copy(way, turn, False).wait_send()


def exact_dot(a, b, dims):
    return lax.dot_general(
        a, b, ((dims[:1], dims[1:]), ((), ())), precision=lax.Precision.HIGHEST, preferred_element_type=F32
    )


def halves(a):
    high = a.astype(BF16)
    return high, (a - high.astype(F32)).astype(BF16)


def close_dot(a, b, dims):
    dot = lambda s, t: lax.dot_general(s, t, ((dims[:1], dims[1:]), ((), ())), preferred_element_type=F32)
    (ah, al), (bh, bl) = halves(a), halves(b)
    return dot(ah, bh) + (dot(ah, bl) + dot(al, bh))


def inverse_factor(a_ref, b_ref):
    lane = lax.broadcasted_iota(jnp.int32, (8, RANK), 1)
    row = lax.broadcasted_iota(jnp.int32, (8, 1), 0)
    b_ref[...] = (
        lax.broadcasted_iota(jnp.int32, (RANK, RANK), 0) == lax.broadcasted_iota(jnp.int32, (RANK, RANK), 1)
    ).astype(F32)

    def panel(t, carry):
        first = pl.multiple_of(t * 8, 8)
        a, b = a_ref[pl.ds(first, 8), :], b_ref[pl.ds(first, 8), :]
        scale, inverse = jnp.zeros((8, 1), F32), jnp.zeros((8, 1), F32)
        for k in range(8):
            column = jnp.sum(jnp.where(lane == first + k, a, 0.0), axis=1, keepdims=True)
            pivot = column[k : k + 1]
            over = 1.0 / pivot
            inverse = jnp.where(row == k, over, inverse)
            scale = jnp.where(row == k, 1.0 / jnp.sqrt(pivot), scale)
            factor = jnp.where(row > k, column * over, 0.0)
            a = a - factor * a[k : k + 1]
            b = b - factor * b[k : k + 1]
        later = jnp.where(lane >= first + 8, a * inverse, 0.0)
        a_ref[...] -= exact_dot(later, a, (0, 0))
        b_ref[...] -= exact_dot(later, b, (0, 0))
        b_ref[pl.ds(first, 8), :] = b * scale
        return carry

    lax.fori_loop(0, RANK // 8, panel, 0)


def tile_place(i):
    return lax.div(i, 16), lax.rem(lax.div(i, 4), 4), lax.rem(i, 4)


def over_columns(body):
    def one(m, carry):
        body(lax.div(m, SIDE), lax.rem(m, SIDE), pl.multiple_of(m * WIDE, WIDE), WIDE)
        return carry

    lax.fori_loop(0, CORES * SIDE - 1, one, 0)
    body(CORES - 1, SIDE - 1, (CORES * SIDE - 1) * WIDE, COLS - (CORES * SIDE - 1) * WIDE)


def over_core_columns(core, body):
    def one(m, carry):
        body(core, m, pl.multiple_of((core * SIDE + m) * WIDE, WIDE), WIDE)
        return carry

    lax.fori_loop(0, SIDE - 1, one, 0)

    @pl.when(core == 0)
    def _():
        body(0, SIDE - 1, (SIDE - 1) * WIDE, WIDE)

    @pl.when(core == 1)
    def _():
        body(CORES - 1, SIDE - 1, (CORES * SIDE - 1) * WIDE, COLS - (CORES * SIDE - 1) * WIDE)


def kernel(
    acts_hbm, g_hbm, f_hbm, q_hbm,
    out_ref, p_out, q_out,
    ga, acts_ref, acts_t, at_ref, ar, acc, qb, qs, tb, fq, pp, p_core, p_one, p_x, p_two, p_y, pe, gram, linv, p_low,
    w, w_core, w_one, w_first, w_two, w_second, w_three, w_z, qa, q_flat,
    load_sem, send_sem, recv_sem, ring_send, ring_recv,
):
    place = Place()
    core, x, y, z = place.core, place.x, place.y, place.z
    sems = Sems(send_sem, recv_sem)
    ring = Ring(place, ga, ring_send, ring_recv)
    part = (core * SIDE + x) * SIDE + y
    part = part - lax.div(part, 31)
    rows_q = q_hbm.at[pl.ds(pl.multiple_of(part * 32, 32), 32)]
    load_acts = pltpu.make_async_copy(acts_hbm, acts_ref, load_sem.at[0])
    own_q = pltpu.make_async_copy(rows_q, qb.at[core, x, y, z], load_sem.at[1])
    load_g = pltpu.make_async_copy(g_hbm, ga.at[z], load_sem.at[2])
    load_f = pltpu.make_async_copy(f_hbm, out_ref, load_sem.at[3])
    for load in (load_acts, own_q, load_g, load_f):
        load.start()
    barrier, others = announce(place)

    load_acts.wait()
    for t in range(16):
        at = slice(t * 128, min((t + 1) * 128, CHIPS * ROWS))
        acts_t[at, :] = acts_ref[:, at].astype(F32).T
    for c in range(CHIPS):
        block = acts_t[c * ROWS : (c + 1) * ROWS, :]
        at_ref[c] = jnp.concatenate([block, jnp.zeros((PAD_ROWS - ROWS, TOK), F32)], axis=0).astype(BF16)
    own_q.wait()
    load_g.wait()
    pl.semaphore_wait(barrier, others)

    done = []

    def both(*steps, meanwhile=None):
        done.extend(steps)
        if meanwhile is not None:
            meanwhile()
        for step in steps:
            step.arrive()

    def gather(name, slot, meanwhile=None):
        both(gather_over(place, name, sems, slot), meanwhile=meanwhile)

    def scatter(name, parts, received, meanwhile=None):
        both(scatter_over(place, name, sems, parts, received), meanwhile=meanwhile)

    def gather_plane(buf, first=None, second=None, third=None):
        half = buf.shape[3] // 2
        a, b = pl.ds(0, half), pl.ds(half, half)
        both(
            gather_over(place, "y", sems, lambda j: buf.at[core, x, j, a]),
            gather_over(place, "x", sems, lambda j: buf.at[core, j, y, b]),
            meanwhile=first,
        )
        both(
            gather_over(place, "x", sems, lambda j: buf.at[core, j, :, a]),
            gather_over(place, "y", sems, lambda j: buf.at[core, :, j, b]),
            meanwhile=second,
        )
        gather("core", lambda j: buf.at[j], third)

    step = gather_over(place, "z", sems, lambda j: qb.at[core, x, y, j])
    acts = Exchange(place, "z", sems, lambda j: at_ref.at[j], lambda s, j: ar.at[j])
    done += [step, acts]
    ring.pump(TA)
    ar[z] = at_ref[z]
    step.arrive()
    gather_plane(qb)

    def place_rows(i, carry):
        for c in range(CHIPS):
            qs[pl.ds(pl.multiple_of(c * 992 + i * 32, 32), 32), :] = qb[(*tile_place(i), c)]
        return carry

    lax.fori_loop(0, 31, place_rows, 0)

    tb[z] = jnp.dot(ga[z], qs[...], preferred_element_type=F32).astype(BF16)

    def feedback_term():
        ring.pump(TB)
        load_f.wait()
        fq[...] = jnp.zeros_like(fq)
        fq[:ROWS, :] = jnp.dot(out_ref[...], qs[...], preferred_element_type=F32)
        acts.arrive()

    gather("z", lambda j: tb.at[j], feedback_term)
    total = fq[...]
    for b in range(CHIPS):
        total += jnp.dot(ar[b], tb[b], preferred_element_type=F32)
    pp[...] = total.reshape(pp.shape)

    scatter("core", pp, p_core)
    p_one[...] = pp[core] + p_core[0]
    scatter("x", p_one, p_x)
    p_two[...] = p_one[x] + p_x[0] + p_x[1] + p_x[2]
    scatter("y", p_two, p_y)
    pe[core, x, y, z] = p_two[y] + p_y[0] + p_y[1] + p_y[2]
    gather("z", lambda j: pe.at[core, x, y, j], lambda: ring.pump(TC))
    gather_plane(pe)

    rows = pe[...].reshape(CHIPS * PAD_ROWS, RANK)
    gram[...] = exact_dot(rows, rows, (0, 0))
    inverse_factor(gram, linv)
    inverse = linv[...]
    for c in range(CHIPS):
        rows = pe[:, :, :, c].reshape(PAD_ROWS, RANK)
        p_low[c] = close_dot(rows, inverse, (1, 1)).astype(BF16)
    ring.pump(TD)

    u = jnp.zeros((RANK, TOK), F32)
    for c in range(CHIPS):
        u += lax.dot_general(p_low[c], at_ref[c], (((0,), (0,)), ((), ())), preferred_element_type=F32)
    u = u.astype(BF16)
    own_p = p_low[z].T[:, :ROWS]

    def fill(at_core, at_x, first, width):
        at = pl.ds(first, width)
        term = jnp.dot(u, ga[z, :, at], preferred_element_type=F32)
        term += jnp.dot(own_p, out_ref[:, at], preferred_element_type=F32)
        term = term.astype(BF16)
        for k in range(width // 128):
            w[at_core, at_x, k // 2, k % 2] = term[:, k * 128 : (k + 1) * 128].reshape(CHIPS, 16, 128)

    def add_blocks(first, *blocks):
        left = jnp.concatenate([ar[b] for b in blocks], axis=1)

        def one(at_core, at_x, start, width):
            at = pl.ds(start, width)
            right = jnp.concatenate([ga[b, :, at] for b in blocks], axis=0)
            term = jnp.dot(left, right, preferred_element_type=F32)
            acc[:, at] = term if first else acc[:, at] + term

        over_columns(one)

    w[CORES - 1, SIDE - 1, SIDE - 1] = jnp.zeros(w.shape[3:], BF16)
    over_core_columns(1 - core, fill)
    scatter("core", w, w_core, lambda: over_core_columns(core, fill))

    def add_core(i, carry):
        w_one[i] = (w[core, i].astype(F32) + w_core[0, i].astype(F32)).astype(BF16)
        return carry

    lax.fori_loop(0, SIDE, add_core, 0)
    both(
        Exchange(place, "x", sems, lambda j: w_one.at[j, :, 0], lambda s, j: w_first.at[0, s - 1]),
        Exchange(place, "y", sems, lambda j: w_one.at[:, j, 1], lambda s, j: w_first.at[1, s - 1]),
        meanwhile=lambda: (ring.arrive(PIECES), add_blocks(True, z, ring.block(0, 1))),
    )

    def sum_of(mine, received):
        return (
            (mine.astype(F32) + received[0].astype(F32))
            + (received[1].astype(F32) + received[2].astype(F32))
        ).astype(BF16)

    w_two[0] = sum_of(w_one[x, :, 0], w_first[0])
    w_two[1] = sum_of(w_one[:, y, 1], w_first[1])
    both(
        Exchange(place, "y", sems, lambda j: w_two.at[0, j], lambda s, j: w_second.at[0, s - 1]),
        Exchange(place, "x", sems, lambda j: w_two.at[1, j], lambda s, j: w_second.at[1, s - 1]),
    )
    total = jnp.stack([sum_of(w_two[0, y], w_second[0]), sum_of(w_two[1, x], w_second[1])])
    for c in range(CHIPS):
        w_three[c] = total[:, c]
    scatter("z", w_three, w_z, lambda: ring.pump(TE))
    mine = w_three[z].astype(F32)
    for c in range(CHIPS - 1):
        mine += w_z[c].astype(F32)
    qa[core, x, y, :, z] = (mine * (1.0 / 32)).astype(BF16)
    gather("z", lambda j: qa.at[core, x, y, :, j], lambda: ring.pump(TF))
    gather_plane(qa)
    ring.arrive(2 * PIECES)
    add_blocks(False, ring.block(1, 1), ring.block(0, 2))
    ring.pump(ring.TURNS - ring.started)

    p_out[...] = close_dot(pe[:, :, :, z].reshape(PAD_ROWS, RANK), inverse, (1, 1))[:ROWS]
    for t in range(9):
        tile = lax.div(z * 31, 4) + t
        block = qa[(*tile_place(lax.div(tile, 2)), lax.rem(tile, 2))].reshape(RANK, 128)
        q_flat[t * 128 : (t + 1) * 128, :] = block.astype(F32).T
    q_out[...] = q_flat[pl.ds(pl.multiple_of(lax.rem(z * 31, 4) * 32, 32), 992), :]

    ring.arrive(3 * PIECES)
    add_blocks(False, ring.block(1, 2), ring.block(0, 3), ring.block(1, 3))
    for step in done:
        step.sent()
    ring.arrive(ring.TURNS)
    last = ring.block(0, 4)
    left = jnp.concatenate([ar[last], -p_low[z]], axis=1)

    def finish(at_core, at_x, first, width):
        at = pl.ds(first, width)
        tiles = qa[at_core, at_x].reshape(WIDE // 128, RANK, 128)
        factor = jnp.concatenate([tiles[k] for k in range(width // 128)], axis=1)
        right = jnp.concatenate([ga[last, :, at], factor], axis=0)
        total = acc[:, at] + jnp.dot(left, right, preferred_element_type=F32)
        out_ref[:, at] = (total[:ROWS] + out_ref[:, at].astype(F32)).astype(BF16)

    over_columns(finish)
    ring.sent()


def whole(acts, g, f, q):
    copies = 128
    vmem = pl.BlockSpec(memory_space=pltpu.VMEM)
    hbm = pl.BlockSpec(memory_space=pltpu.HBM)
    tile = (CHIPS, 16, 128)
    return pl.pallas_call(
        kernel,
        out_shape=(
            jax.ShapeDtypeStruct((ROWS, COLS), BF16),
            jax.ShapeDtypeStruct((ROWS, RANK), F32),
            jax.ShapeDtypeStruct((992, RANK), F32),
        ),
        in_specs=[hbm, hbm, hbm, hbm],
        out_specs=(vmem, vmem, vmem),
        scratch_shapes=[
            pltpu.VMEM((CHIPS, TOK, COLS), BF16),
            pltpu.VMEM((TOK, CHIPS * ROWS), BF16),
            pltpu.VMEM((CHIPS * ROWS, TOK), F32),
            pltpu.VMEM((CHIPS, PAD_ROWS, TOK), BF16),
            pltpu.VMEM((CHIPS, PAD_ROWS, TOK), BF16),
            pltpu.VMEM((PAD_ROWS, COLS), F32),
            pltpu.VMEM((CORES, SIDE, SIDE, CHIPS, 32, RANK), BF16),
            pltpu.VMEM((COLS, RANK), BF16),
            pltpu.VMEM((CHIPS, TOK, RANK), BF16),
            pltpu.VMEM((PAD_ROWS, RANK), F32),
            pltpu.VMEM((CORES, SIDE, SIDE, 8, RANK), F32),
            pltpu.VMEM((1, SIDE, SIDE, 8, RANK), F32),
            pltpu.VMEM((SIDE, SIDE, 8, RANK), F32),
            pltpu.VMEM((3, SIDE, 8, RANK), F32),
            pltpu.VMEM((SIDE, 8, RANK), F32),
            pltpu.VMEM((3, 8, RANK), F32),
            pltpu.VMEM((CORES, SIDE, SIDE, CHIPS, 8, RANK), F32),
            pltpu.VMEM((RANK, RANK), F32),
            pltpu.VMEM((RANK, RANK), F32),
            pltpu.VMEM((CHIPS, PAD_ROWS, RANK), BF16),
            pltpu.VMEM((CORES, SIDE, SIDE, 2, *tile), BF16),
            pltpu.VMEM((1, SIDE, SIDE, 2, *tile), BF16),
            pltpu.VMEM((SIDE, SIDE, 2, *tile), BF16),
            pltpu.VMEM((2, 3, SIDE, *tile), BF16),
            pltpu.VMEM((2, SIDE, *tile), BF16),
            pltpu.VMEM((2, 3, *tile), BF16),
            pltpu.VMEM((CHIPS, 2, 16, 128), BF16),
            pltpu.VMEM((CHIPS - 1, 2, 16, 128), BF16),
            pltpu.VMEM((CORES, SIDE, SIDE, 2, *tile), BF16),
            pltpu.VMEM((9 * 128, RANK), F32),
            pltpu.SemaphoreType.DMA((4,)),
            pltpu.SemaphoreType.DMA((copies,)),
            pltpu.SemaphoreType.DMA((copies,)),
            pltpu.SemaphoreType.DMA((2, Ring.TURNS)),
            pltpu.SemaphoreType.DMA((2, Ring.TURNS)),
        ],
        compiler_params=pltpu.CompilerParams(
            collective_id=0, has_side_effects=True, vmem_limit_bytes=VMEM_MIB * 2**20
        ),
        cost_estimate=pl.CostEstimate(flops=10**10, bytes_accessed=30 * 10**6, transcendentals=0),
    )(acts, g, f, q)


def local(activations, hidden_grad, feedback, q_start):
    return whole(activations, hidden_grad, feedback, q_start)


def solution(mesh):
    in_specs = (
        P(("node", "chip"), None),
        P(("node", "chip"), None),
        P(("node", "chip"), None),
        P("chip", None),
    )
    out_specs = (P(("node", "chip"), None), P("chip", None), P("chip", None))
    return jax.shard_map(local, mesh=mesh, in_specs=in_specs, out_specs=out_specs, check_vma=False)
```

```python
import jax
import jax.numpy as jnp
from jax import lax
from jax.experimental import pallas as pl
from jax.experimental.pallas import tpu as pltpu
from jax.sharding import PartitionSpec as P

MESH = pl.DeviceIdType.MESH
F32, BF16 = jnp.float32, jnp.bfloat16
CHIPS, SIDE, CORES = 8, 4, 2
ROWS, COLS, RANK, TOK = 248, 7936, 128, 128
PAD_ROWS = 256
WIDE = 1024
VMEM_MIB = 45
TA, TB, TC, TD, TE, TF = 5, 1, 7, 4, 1, 8
PIECES = 8
TILES = (8, 8, 8, 7, 7, 8, 8, 8)


class Place:
    def __init__(self):
        node = lax.axis_index("node")
        self.core = lax.rem(node, CORES)
        self.x = lax.rem(lax.div(node, CORES), SIDE)
        self.y = lax.div(node, CORES * SIDE)
        self.z = lax.axis_index("chip")

    def node(self, y, x, core):
        return (y * SIDE + x) * CORES + core

    def axis(self, name):
        if name == "z":
            return CHIPS, self.z, lambda j: {"chip": j}
        if name == "y":
            return SIDE, self.y, lambda j: {"node": self.node(j, self.x, self.core)}
        if name == "x":
            return SIDE, self.x, lambda j: {"node": self.node(self.y, j, self.core)}
        return CORES, self.core, lambda j: {"node": self.node(self.y, self.x, j)}


def announce(place):
    sem = pltpu.get_barrier_semaphore()
    count = 0
    for name in ("z", "y", "x", "core"):
        size, own, device = place.axis(name)
        for step in range(1, size):
            pl.semaphore_signal(
                sem, inc=1, device_id=device(lax.rem(own + step, size)), device_id_type=MESH
            )
            count += 1
    return sem, count


class Sems:
    def __init__(self, send, recv):
        self.send, self.recv, self.used = send, recv, 0

    def take(self):
        self.used += 1
        return self.send.at[self.used - 1], self.recv.at[self.used - 1]


class Exchange:
    def __init__(self, place, name, sems, source, landing):
        size, own, device = place.axis(name)
        self.copies = []
        for step in range(1, size):
            to, of = lax.rem(own + step, size), lax.rem(own + size - step, size)
            send, recv = sems.take()
            self.copies.append(
                (
                    pltpu.make_async_remote_copy(
                        src_ref=source(to),
                        dst_ref=landing(step, own),
                        send_sem=send,
                        recv_sem=recv,
                        device_id=device(to),
                        device_id_type=MESH,
                    ),
                    pltpu.make_async_remote_copy(
                        src_ref=landing(step, of),
                        dst_ref=landing(step, of),
                        send_sem=send,
                        recv_sem=recv,
                        device_id=device(to),
                        device_id_type=MESH,
                    ),
                )
            )
        for out, _ in self.copies:
            out.start()

    def arrive(self):
        for _, inward in self.copies:
            inward.wait_recv()

    def sent(self):
        for out, _ in self.copies:
            out.wait_send()


def gather_over(place, name, sems, slot):
    own = place.axis(name)[1]
    return Exchange(place, name, sems, lambda j: slot(own), lambda step, j: slot(j))


def scatter_over(place, name, sems, parts, received):
    return Exchange(
        place, name, sems, lambda j: parts.at[j], lambda step, j: received.at[step - 1]
    )


def tiles_of(piece):
    first = sum(TILES[:piece])
    return range(first, first + TILES[piece])


def columns_of(piece):
    return pl.ds(tiles_of(piece)[0] * 128, TILES[piece] * 128)


class Ring:
    TURNS = 3 * PIECES + PIECES // 2

    def __init__(self, place, g_ref, send, recv):
        self.z, self.g, self.send, self.recv = place.z, g_ref, send, recv
        self.device = place.axis("z")[2]
        self.started = self.arrived = 0

    def block(self, way, hops):
        return lax.rem(self.z + (CHIPS - hops if way == 0 else hops), CHIPS)

    def copy(self, way, turn, received):
        hop, i = turn // PIECES + 1, turn % PIECES
        piece = i if way == 0 else PIECES - 1 - i
        view = self.g.at[self.block(way, hop if received else hop - 1), :, columns_of(piece)]
        to = lax.rem(self.z + (1 if way == 0 else CHIPS - 1), CHIPS)
        return pltpu.make_async_remote_copy(
            src_ref=view,
            dst_ref=view,
            send_sem=self.send.at[way, turn],
            recv_sem=self.recv.at[way, turn],
            device_id=self.device(to),
            device_id_type=MESH,
        )

    def arrive(self, turns):
        while self.arrived < turns:
            for way in range(2):
                self.copy(way, self.arrived, True).wait_recv()
            self.arrived += 1

    def pump(self, turns):
        for _ in range(turns):
            self.arrive(self.started + 1 - PIECES)
            for way in range(2):
                self.copy(way, self.started, False).start()
            self.started += 1

    def sent(self):
        for turn in range(self.TURNS):
            for way in range(2):
                self.copy(way, turn, False).wait_send()


def exact_dot(a, b, dims):
    return lax.dot_general(
        a, b, ((dims[:1], dims[1:]), ((), ())), precision=lax.Precision.HIGHEST, preferred_element_type=F32
    )


def halves(a):
    high = a.astype(BF16)
    return high, (a - high.astype(F32)).astype(BF16)


def close_dot(a, b, dims):
    dot = lambda s, t: lax.dot_general(s, t, ((dims[:1], dims[1:]), ((), ())), preferred_element_type=F32)
    (ah, al), (bh, bl) = halves(a), halves(b)
    return dot(ah, bh) + (dot(ah, bl) + dot(al, bh))


def inverse_factor(a_ref, b_ref):
    lane = lax.broadcasted_iota(jnp.int32, (8, RANK), 1)
    row = lax.broadcasted_iota(jnp.int32, (8, 1), 0)
    b_ref[...] = (
        lax.broadcasted_iota(jnp.int32, (RANK, RANK), 0) == lax.broadcasted_iota(jnp.int32, (RANK, RANK), 1)
    ).astype(F32)

    def panel(t, carry):
        first = pl.multiple_of(t * 8, 8)
        a, b = a_ref[pl.ds(first, 8), :], b_ref[pl.ds(first, 8), :]
        scale, inverse = jnp.zeros((8, 1), F32), jnp.zeros((8, 1), F32)
        for k in range(8):
            column = jnp.sum(jnp.where(lane == first + k, a, 0.0), axis=1, keepdims=True)
            pivot = column[k : k + 1]
            over = 1.0 / pivot
            inverse = jnp.where(row == k, over, inverse)
            scale = jnp.where(row == k, 1.0 / jnp.sqrt(pivot), scale)
            factor = jnp.where(row > k, column * over, 0.0)
            a = a - factor * a[k : k + 1]
            b = b - factor * b[k : k + 1]
        later = jnp.where(lane >= first + 8, a * inverse, 0.0)
        a_ref[...] -= exact_dot(later, a, (0, 0))
        b_ref[...] -= exact_dot(later, b, (0, 0))
        b_ref[pl.ds(first, 8), :] = b * scale
        return carry

    lax.fori_loop(0, RANK // 8, panel, 0)


def tile_place(i):
    return lax.div(i, 16), lax.rem(lax.div(i, 4), 4), lax.rem(i, 4)


def over_columns(body):
    def one(m, carry):
        body(lax.div(m, SIDE), lax.rem(m, SIDE), pl.multiple_of(m * WIDE, WIDE), WIDE)
        return carry

    lax.fori_loop(0, CORES * SIDE - 1, one, 0)
    body(CORES - 1, SIDE - 1, (CORES * SIDE - 1) * WIDE, COLS - (CORES * SIDE - 1) * WIDE)


def over_core_columns(core, body):
    def one(m, carry):
        body(core, m, pl.multiple_of((core * SIDE + m) * WIDE, WIDE), WIDE)
        return carry

    lax.fori_loop(0, SIDE - 1, one, 0)

    @pl.when(core == 0)
    def _():
        body(0, SIDE - 1, (SIDE - 1) * WIDE, WIDE)

    @pl.when(core == 1)
    def _():
        body(CORES - 1, SIDE - 1, (CORES * SIDE - 1) * WIDE, COLS - (CORES * SIDE - 1) * WIDE)


def kernel(
    at_hbm, g_hbm, f_hbm, q_hbm,
    out_ref, p_out, q_out,
    ga, acts_t, at_ref, ar, acc, qb, qs, pp, p_core, p_one, p_first, p_two, p_second, p_three, p_z, pe, gram, linv,
    p_low,
    w, w_core, w_one, w_first, w_two, w_second, w_three, w_z, qa, q_flat,
    load_sem, send_sem, recv_sem, ring_send, ring_recv,
):
    place = Place()
    core, x, y, z = place.core, place.x, place.y, place.z
    sems = Sems(send_sem, recv_sem)
    ring = Ring(place, ga, ring_send, ring_recv)
    part = (core * SIDE + x) * SIDE + y
    part = part - lax.div(part, 31)
    rows_q = q_hbm.at[pl.ds(pl.multiple_of(part * 32, 32), 32)]
    load_acts = pltpu.make_async_copy(at_hbm, acts_t, load_sem.at[0])
    own_q = pltpu.make_async_copy(rows_q, qb.at[core, x, y, z], load_sem.at[1])
    load_g = pltpu.make_async_copy(g_hbm, ga.at[z], load_sem.at[2])
    load_f = pltpu.make_async_copy(f_hbm, out_ref, load_sem.at[3])
    for load in (load_acts, own_q, load_g, load_f):
        load.start()
    barrier, others = announce(place)

    load_acts.wait()
    rows = acts_t[...].astype(F32)
    for c in range(CHIPS):
        block = rows[c * ROWS : (c + 1) * ROWS]
        at_ref[c] = jnp.concatenate([block, jnp.zeros((PAD_ROWS - ROWS, TOK), F32)], axis=0).astype(BF16)
    own_q.wait()
    load_g.wait()
    pl.semaphore_wait(barrier, others)

    done = []

    def both(*steps, meanwhile=None):
        done.extend(steps)
        if meanwhile is not None:
            meanwhile()
        for step in steps:
            step.arrive()

    def gather(name, slot, meanwhile=None):
        both(gather_over(place, name, sems, slot), meanwhile=meanwhile)

    def scatter(name, parts, received, meanwhile=None):
        both(scatter_over(place, name, sems, parts, received), meanwhile=meanwhile)

    def gather_plane(buf, first=None, second=None, third=None):
        half = buf.shape[3] // 2
        a, b = pl.ds(0, half), pl.ds(half, half)
        both(
            gather_over(place, "y", sems, lambda j: buf.at[core, x, j, a]),
            gather_over(place, "x", sems, lambda j: buf.at[core, j, y, b]),
            meanwhile=first,
        )
        both(
            gather_over(place, "x", sems, lambda j: buf.at[core, j, :, a]),
            gather_over(place, "y", sems, lambda j: buf.at[core, :, j, b]),
            meanwhile=second,
        )
        gather("core", lambda j: buf.at[j], third)

    step = gather_over(place, "z", sems, lambda j: qb.at[core, x, y, j])
    acts = Exchange(place, "z", sems, lambda j: at_ref.at[j], lambda s, j: ar.at[j])
    done += [step, acts]
    ring.pump(TA)
    ar[z] = at_ref[z]
    step.arrive()
    gather_plane(qb)

    def place_rows(i, carry):
        for c in range(CHIPS):
            qs[pl.ds(pl.multiple_of(c * 992 + i * 32, 32), 32), :] = qb[(*tile_place(i), c)]
        return carry

    lax.fori_loop(0, 31, place_rows, 0)

    tokens = jnp.dot(ga[z], qs[...], preferred_element_type=F32).astype(BF16)
    for c in range(CHIPS):
        term = jnp.dot(at_ref[c], tokens, preferred_element_type=F32)
        pp[:, :, :, c] = term.reshape(CORES, SIDE, SIDE, 8, RANK)
    load_f.wait()
    term = jnp.dot(out_ref[...], qs[...], preferred_element_type=F32)
    term = jnp.concatenate([term, jnp.zeros((PAD_ROWS - ROWS, RANK), F32)], axis=0)
    pp[:, :, :, z] = pp[:, :, :, z] + term.reshape(CORES, SIDE, SIDE, 8, RANK)

    scatter("core", pp, p_core)
    p_one[...] = pp[core] + p_core[0]
    low, high = pl.ds(0, CHIPS // 2), pl.ds(CHIPS // 2, CHIPS // 2)
    both(
        Exchange(place, "x", sems, lambda j: p_one.at[j, :, low], lambda s, j: p_first.at[0, s - 1]),
        Exchange(place, "y", sems, lambda j: p_one.at[:, j, high], lambda s, j: p_first.at[1, s - 1]),
    )
    p_two[0] = (p_one[x, :, low] + p_first[0, 0]) + (p_first[0, 1] + p_first[0, 2])
    p_two[1] = (p_one[:, y, high] + p_first[1, 0]) + (p_first[1, 1] + p_first[1, 2])
    both(
        Exchange(place, "y", sems, lambda j: p_two.at[0, j], lambda s, j: p_second.at[0, s - 1]),
        Exchange(place, "x", sems, lambda j: p_two.at[1, j], lambda s, j: p_second.at[1, s - 1]),
    )
    p_three[low] = (p_two[0, y] + p_second[0, 0]) + (p_second[0, 1] + p_second[0, 2])
    p_three[high] = (p_two[1, x] + p_second[1, 0]) + (p_second[1, 1] + p_second[1, 2])
    scatter("z", p_three, p_z, lambda: ring.pump(TB))
    total = p_three[z]
    for c in range(CHIPS - 1):
        total += p_z[c]
    pe[core, x, y, z] = total
    gather("z", lambda j: pe.at[core, x, y, j], lambda: ring.pump(TC))
    gather_plane(pe)

    rows = pe[...].reshape(CHIPS * PAD_ROWS, RANK)
    gram[...] = exact_dot(rows, rows, (0, 0))
    inverse_factor(gram, linv)
    inverse = linv[...]
    for c in range(CHIPS):
        rows = pe[:, :, :, c].reshape(PAD_ROWS, RANK)
        p_low[c] = close_dot(rows, inverse, (1, 1)).astype(BF16)
    ring.pump(TD)

    u = jnp.zeros((RANK, TOK), F32)
    for c in range(CHIPS):
        u += lax.dot_general(p_low[c], at_ref[c], (((0,), (0,)), ((), ())), preferred_element_type=F32)
    u = u.astype(BF16)
    own_p = p_low[z].T[:, :ROWS]

    def fill(at_core, at_x, first, width):
        at = pl.ds(first, width)
        term = jnp.dot(u, ga[z, :, at], preferred_element_type=F32)
        term += jnp.dot(own_p, out_ref[:, at], preferred_element_type=F32)
        term = term.astype(BF16)
        for k in range(width // 128):
            w[at_core, at_x, k // 2, k % 2] = term[:, k * 128 : (k + 1) * 128].reshape(CHIPS, 16, 128)

    def add_blocks(first, *blocks):
        left = jnp.concatenate([ar[b] for b in blocks], axis=1)

        def one(at_core, at_x, start, width):
            at = pl.ds(start, width)
            right = jnp.concatenate([ga[b, :, at] for b in blocks], axis=0)
            term = jnp.dot(left, right, preferred_element_type=F32)
            acc[:, at] = term if first else acc[:, at] + term

        over_columns(one)

    w[CORES - 1, SIDE - 1, SIDE - 1] = jnp.zeros(w.shape[3:], BF16)
    over_core_columns(1 - core, fill)
    scatter("core", w, w_core, lambda: over_core_columns(core, fill))

    def add_core(i, carry):
        w_one[i] = (w[core, i].astype(F32) + w_core[0, i].astype(F32)).astype(BF16)
        return carry

    lax.fori_loop(0, SIDE, add_core, 0)
    both(
        Exchange(place, "x", sems, lambda j: w_one.at[j, :, 0], lambda s, j: w_first.at[0, s - 1]),
        Exchange(place, "y", sems, lambda j: w_one.at[:, j, 1], lambda s, j: w_first.at[1, s - 1]),
        meanwhile=lambda: (acts.arrive(), ring.arrive(PIECES), add_blocks(True, z, ring.block(0, 1))),
    )

    def sum_of(mine, received):
        return (
            (mine.astype(F32) + received[0].astype(F32))
            + (received[1].astype(F32) + received[2].astype(F32))
        ).astype(BF16)

    w_two[0] = sum_of(w_one[x, :, 0], w_first[0])
    w_two[1] = sum_of(w_one[:, y, 1], w_first[1])
    both(
        Exchange(place, "y", sems, lambda j: w_two.at[0, j], lambda s, j: w_second.at[0, s - 1]),
        Exchange(place, "x", sems, lambda j: w_two.at[1, j], lambda s, j: w_second.at[1, s - 1]),
    )
    total = jnp.stack([sum_of(w_two[0, y], w_second[0]), sum_of(w_two[1, x], w_second[1])])
    for c in range(CHIPS):
        w_three[c] = total[:, c]
    scatter("z", w_three, w_z, lambda: ring.pump(TE))
    mine = w_three[z].astype(F32)
    for c in range(CHIPS - 1):
        mine += w_z[c].astype(F32)
    qa[core, x, y, :, z] = (mine * (1.0 / 32)).astype(BF16)
    gather("z", lambda j: qa.at[core, x, y, :, j], lambda: ring.pump(TF))
    gather_plane(qa)
    ring.arrive(2 * PIECES)
    add_blocks(False, ring.block(1, 1), ring.block(0, 2))
    ring.pump(ring.TURNS - ring.started)

    p_out[...] = close_dot(pe[:, :, :, z].reshape(PAD_ROWS, RANK), inverse, (1, 1))[:ROWS]
    for t in range(9):
        tile = lax.div(z * 31, 4) + t
        block = qa[(*tile_place(lax.div(tile, 2)), lax.rem(tile, 2))].reshape(RANK, 128)
        q_flat[t * 128 : (t + 1) * 128, :] = block.astype(F32).T
    q_out[...] = q_flat[pl.ds(pl.multiple_of(lax.rem(z * 31, 4) * 32, 32), 992), :]

    ring.arrive(3 * PIECES)
    add_blocks(False, ring.block(1, 2), ring.block(0, 3), ring.block(1, 3))
    for step in done:
        step.sent()
    last = ring.block(0, 4)
    left = jnp.concatenate([ar[last], -p_low[z]], axis=1)

    def finish(piece):
        at = columns_of(piece)
        tiles = [qa[t // 32, t // 8 % 4, t // 2 % 4, t % 2].reshape(RANK, 128) for t in tiles_of(piece)]
        right = jnp.concatenate([ga[last, :, at], jnp.concatenate(tiles, axis=1)], axis=0)
        total = acc[:, at] + jnp.dot(left, right, preferred_element_type=F32)
        out_ref[:, at] = (total[:ROWS] + out_ref[:, at].astype(F32)).astype(BF16)

    for i in range(PIECES // 2):
        ring.arrive(3 * PIECES + i + 1)
        finish(i)
        finish(PIECES - 1 - i)
    ring.sent()


def whole(at, g, f, q):
    copies = 128
    vmem = pl.BlockSpec(memory_space=pltpu.VMEM)
    hbm = pl.BlockSpec(memory_space=pltpu.HBM)
    tile = (CHIPS, 16, 128)
    return pl.pallas_call(
        kernel,
        out_shape=(
            jax.ShapeDtypeStruct((ROWS, COLS), BF16),
            jax.ShapeDtypeStruct((ROWS, RANK), F32),
            jax.ShapeDtypeStruct((992, RANK), F32),
        ),
        in_specs=[hbm, hbm, hbm, hbm],
        out_specs=(vmem, vmem, vmem),
        scratch_shapes=[
            pltpu.VMEM((CHIPS, TOK, COLS), BF16),
            pltpu.VMEM((CHIPS * ROWS, TOK), BF16),
            pltpu.VMEM((CHIPS, PAD_ROWS, TOK), BF16),
            pltpu.VMEM((CHIPS, PAD_ROWS, TOK), BF16),
            pltpu.VMEM((PAD_ROWS, COLS), F32),
            pltpu.VMEM((CORES, SIDE, SIDE, CHIPS, 32, RANK), BF16),
            pltpu.VMEM((COLS, RANK), BF16),
            pltpu.VMEM((CORES, SIDE, SIDE, CHIPS, 8, RANK), F32),
            pltpu.VMEM((1, SIDE, SIDE, CHIPS, 8, RANK), F32),
            pltpu.VMEM((SIDE, SIDE, CHIPS, 8, RANK), F32),
            pltpu.VMEM((2, 3, SIDE, CHIPS // 2, 8, RANK), F32),
            pltpu.VMEM((2, SIDE, CHIPS // 2, 8, RANK), F32),
            pltpu.VMEM((2, 3, CHIPS // 2, 8, RANK), F32),
            pltpu.VMEM((CHIPS, 8, RANK), F32),
            pltpu.VMEM((CHIPS - 1, 8, RANK), F32),
            pltpu.VMEM((CORES, SIDE, SIDE, CHIPS, 8, RANK), F32),
            pltpu.VMEM((RANK, RANK), F32),
            pltpu.VMEM((RANK, RANK), F32),
            pltpu.VMEM((CHIPS, PAD_ROWS, RANK), BF16),
            pltpu.VMEM((CORES, SIDE, SIDE, 2, *tile), BF16),
            pltpu.VMEM((1, SIDE, SIDE, 2, *tile), BF16),
            pltpu.VMEM((SIDE, SIDE, 2, *tile), BF16),
            pltpu.VMEM((2, 3, SIDE, *tile), BF16),
            pltpu.VMEM((2, SIDE, *tile), BF16),
            pltpu.VMEM((2, 3, *tile), BF16),
            pltpu.VMEM((CHIPS, 2, 16, 128), BF16),
            pltpu.VMEM((CHIPS - 1, 2, 16, 128), BF16),
            pltpu.VMEM((CORES, SIDE, SIDE, 2, *tile), BF16),
            pltpu.VMEM((9 * 128, RANK), F32),
            pltpu.SemaphoreType.DMA((4,)),
            pltpu.SemaphoreType.DMA((copies,)),
            pltpu.SemaphoreType.DMA((copies,)),
            pltpu.SemaphoreType.DMA((2, Ring.TURNS)),
            pltpu.SemaphoreType.DMA((2, Ring.TURNS)),
        ],
        compiler_params=pltpu.CompilerParams(
            collective_id=0, has_side_effects=True, vmem_limit_bytes=VMEM_MIB * 2**20
        ),
        cost_estimate=pl.CostEstimate(flops=10**10, bytes_accessed=30 * 10**6, transcendentals=0),
    )(at, g, f, q)


def local(activations, hidden_grad, feedback, q_start):
    here = lambda a: pltpu.with_memory_space_constraint(a, pltpu.HBM)
    return whole(here(activations.T), here(hidden_grad), here(feedback), here(q_start))


def solution(mesh):
    in_specs = (
        P(("node", "chip"), None),
        P(("node", "chip"), None),
        P(("node", "chip"), None),
        P("chip", None),
    )
    out_specs = (P(("node", "chip"), None), P("chip", None), P("chip", None))
    return jax.shard_map(local, mesh=mesh, in_specs=in_specs, out_specs=out_specs, check_vma=False)
```

```python
import jax
import jax.numpy as jnp
from jax import lax
from jax.experimental import pallas as pl
from jax.experimental.pallas import tpu as pltpu
from jax.sharding import PartitionSpec as P

MESH = pl.DeviceIdType.MESH
F32, BF16 = jnp.float32, jnp.bfloat16
CHIPS, SIDE, CORES = 8, 4, 2
ROWS, COLS, RANK, TOK = 248, 7936, 128, 128
PAD_ROWS = 256
WIDE = 1024
VMEM_MIB = 45
TA, TB, TC, TD, TE, TF = 5, 1, 7, 4, 1, 8
PIECES = 8
TILES = (8, 8, 8, 7, 7, 8, 8, 8)


class Place:
    def __init__(self):
        node = lax.axis_index("node")
        self.core = lax.rem(node, CORES)
        self.x = lax.rem(lax.div(node, CORES), SIDE)
        self.y = lax.div(node, CORES * SIDE)
        self.z = lax.axis_index("chip")

    def node(self, y, x, core):
        return (y * SIDE + x) * CORES + core

    def axis(self, name):
        if name == "z":
            return CHIPS, self.z, lambda j: {"chip": j}
        if name == "y":
            return SIDE, self.y, lambda j: {"node": self.node(j, self.x, self.core)}
        if name == "x":
            return SIDE, self.x, lambda j: {"node": self.node(self.y, j, self.core)}
        return CORES, self.core, lambda j: {"node": self.node(self.y, self.x, j)}


def announce(place):
    sem = pltpu.get_barrier_semaphore()
    count = 0
    for name in ("z", "y", "x", "core"):
        size, own, device = place.axis(name)
        for step in range(1, size):
            pl.semaphore_signal(
                sem, inc=1, device_id=device(lax.rem(own + step, size)), device_id_type=MESH
            )
            count += 1
    return sem, count


class Sems:
    def __init__(self, send, recv):
        self.send, self.recv, self.used = send, recv, 0

    def take(self):
        self.used += 1
        return self.send.at[self.used - 1], self.recv.at[self.used - 1]


class Exchange:
    def __init__(self, place, name, sems, source, landing):
        size, own, device = place.axis(name)
        self.copies = []
        for step in range(1, size):
            to, of = lax.rem(own + step, size), lax.rem(own + size - step, size)
            send, recv = sems.take()
            self.copies.append(
                (
                    pltpu.make_async_remote_copy(
                        src_ref=source(to),
                        dst_ref=landing(step, own),
                        send_sem=send,
                        recv_sem=recv,
                        device_id=device(to),
                        device_id_type=MESH,
                    ),
                    pltpu.make_async_remote_copy(
                        src_ref=landing(step, of),
                        dst_ref=landing(step, of),
                        send_sem=send,
                        recv_sem=recv,
                        device_id=device(to),
                        device_id_type=MESH,
                    ),
                )
            )
        for out, _ in self.copies:
            out.start()

    def arrive(self):
        for _, inward in self.copies:
            inward.wait_recv()

    def sent(self):
        for out, _ in self.copies:
            out.wait_send()


def gather_over(place, name, sems, slot):
    own = place.axis(name)[1]
    return Exchange(place, name, sems, lambda j: slot(own), lambda step, j: slot(j))


def scatter_over(place, name, sems, parts, received):
    return Exchange(
        place, name, sems, lambda j: parts.at[j], lambda step, j: received.at[step - 1]
    )


def tiles_of(piece):
    first = sum(TILES[:piece])
    return range(first, first + TILES[piece])


def columns_of(piece):
    return pl.ds(tiles_of(piece)[0] * 128, TILES[piece] * 128)


class Ring:
    TURNS = 3 * PIECES + PIECES // 2

    def __init__(self, place, g_ref, send, recv):
        self.z, self.g, self.send, self.recv = place.z, g_ref, send, recv
        self.device = place.axis("z")[2]
        self.started = self.arrived = 0

    def block(self, way, hops):
        return lax.rem(self.z + (CHIPS - hops if way == 0 else hops), CHIPS)

    def copy(self, way, turn, received):
        hop, i = turn // PIECES + 1, turn % PIECES
        piece = i if way == 0 else PIECES - 1 - i
        view = self.g.at[self.block(way, hop if received else hop - 1), :, columns_of(piece)]
        to = lax.rem(self.z + (1 if way == 0 else CHIPS - 1), CHIPS)
        return pltpu.make_async_remote_copy(
            src_ref=view,
            dst_ref=view,
            send_sem=self.send.at[way, turn],
            recv_sem=self.recv.at[way, turn],
            device_id=self.device(to),
            device_id_type=MESH,
        )

    def arrive(self, turns):
        while self.arrived < turns:
            for way in range(2):
                self.copy(way, self.arrived, True).wait_recv()
            self.arrived += 1

    def pump(self, turns):
        for _ in range(turns):
            self.arrive(self.started + 1 - PIECES)
            for way in range(2):
                self.copy(way, self.started, False).start()
            self.started += 1

    def sent(self):
        for turn in range(self.TURNS):
            for way in range(2):
                self.copy(way, turn, False).wait_send()


def exact_dot(a, b, dims):
    return lax.dot_general(
        a, b, ((dims[:1], dims[1:]), ((), ())), precision=lax.Precision.HIGHEST, preferred_element_type=F32
    )


def halves(a):
    high = a.astype(BF16)
    return high, (a - high.astype(F32)).astype(BF16)


def close_dot(a, b, dims):
    dot = lambda s, t: lax.dot_general(s, t, ((dims[:1], dims[1:]), ((), ())), preferred_element_type=F32)
    (ah, al), (bh, bl) = halves(a), halves(b)
    return dot(ah, bh) + (dot(ah, bl) + dot(al, bh))


def inverse_factor(a_ref, b_ref):
    lane = lax.broadcasted_iota(jnp.int32, (8, RANK), 1)
    row = lax.broadcasted_iota(jnp.int32, (8, 1), 0)
    b_ref[...] = (
        lax.broadcasted_iota(jnp.int32, (RANK, RANK), 0) == lax.broadcasted_iota(jnp.int32, (RANK, RANK), 1)
    ).astype(F32)

    def panel(t, carry):
        first = pl.multiple_of(t * 8, 8)
        a, b = a_ref[pl.ds(first, 8), :], b_ref[pl.ds(first, 8), :]
        scale, inverse = jnp.zeros((8, 1), F32), jnp.zeros((8, 1), F32)
        for k in range(8):
            column = jnp.sum(jnp.where(lane == first + k, a, 0.0), axis=1, keepdims=True)
            pivot = column[k : k + 1]
            over = 1.0 / pivot
            inverse = jnp.where(row == k, over, inverse)
            scale = jnp.where(row == k, 1.0 / jnp.sqrt(pivot), scale)
            factor = jnp.where(row > k, column * over, 0.0)
            a = a - factor * a[k : k + 1]
            b = b - factor * b[k : k + 1]
        later = jnp.where(lane >= first + 8, a * inverse, 0.0)
        a_ref[...] -= exact_dot(later, a, (0, 0))
        b_ref[...] -= exact_dot(later, b, (0, 0))
        b_ref[pl.ds(first, 8), :] = b * scale
        return carry

    lax.fori_loop(0, RANK // 8, panel, 0)


def tile_place(i):
    return lax.div(i, 16), lax.rem(lax.div(i, 4), 4), lax.rem(i, 4)


def over_columns(body):
    def one(m, carry):
        body(lax.div(m, SIDE), lax.rem(m, SIDE), pl.multiple_of(m * WIDE, WIDE), WIDE)
        return carry

    lax.fori_loop(0, CORES * SIDE - 1, one, 0)
    body(CORES - 1, SIDE - 1, (CORES * SIDE - 1) * WIDE, COLS - (CORES * SIDE - 1) * WIDE)


def over_core_columns(core, body):
    def one(m, carry):
        body(core, m, pl.multiple_of((core * SIDE + m) * WIDE, WIDE), WIDE)
        return carry

    lax.fori_loop(0, SIDE - 1, one, 0)

    @pl.when(core == 0)
    def _():
        body(0, SIDE - 1, (SIDE - 1) * WIDE, WIDE)

    @pl.when(core == 1)
    def _():
        body(CORES - 1, SIDE - 1, (CORES * SIDE - 1) * WIDE, COLS - (CORES * SIDE - 1) * WIDE)


def kernel(
    at_hbm, g_hbm, f_hbm, q_hbm,
    out_ref, p_out, q_out,
    ga, acts_t, at_ref, ar, acc, qb, qs, pp, p_core, p_one, p_first, p_two, p_second, p_three, p_z, pe, gram, linv,
    p_low,
    w, w_core, w_one, w_first, w_two, w_second, w_three, w_z, qa, q_flat,
    load_sem, send_sem, recv_sem, ring_send, ring_recv,
):
    place = Place()
    core, x, y, z = place.core, place.x, place.y, place.z
    sems = Sems(send_sem, recv_sem)
    ring = Ring(place, ga, ring_send, ring_recv)
    part = (core * SIDE + x) * SIDE + y
    part = part - lax.div(part, 31)
    rows_q = q_hbm.at[pl.ds(pl.multiple_of(part * 32, 32), 32)]
    load_acts = pltpu.make_async_copy(at_hbm, acts_t, load_sem.at[0])
    own_q = pltpu.make_async_copy(rows_q, qb.at[core, x, y, z], load_sem.at[1])
    load_g = pltpu.make_async_copy(g_hbm, ga.at[z], load_sem.at[2])
    load_f = pltpu.make_async_copy(f_hbm, out_ref, load_sem.at[3])
    for load in (load_acts, own_q, load_g, load_f):
        load.start()
    barrier, others = announce(place)

    own_q.wait()
    load_g.wait()
    pl.semaphore_wait(barrier, others)

    done = []

    def both(*steps, meanwhile=None):
        done.extend(steps)
        if meanwhile is not None:
            meanwhile()
        for step in steps:
            step.arrive()

    def gather(name, slot, meanwhile=None):
        both(gather_over(place, name, sems, slot), meanwhile=meanwhile)

    def scatter(name, parts, received, meanwhile=None):
        both(scatter_over(place, name, sems, parts, received), meanwhile=meanwhile)

    def gather_plane(buf, first=None, second=None, third=None):
        half = buf.shape[3] // 2
        a, b = pl.ds(0, half), pl.ds(half, half)
        both(
            gather_over(place, "y", sems, lambda j: buf.at[core, x, j, a]),
            gather_over(place, "x", sems, lambda j: buf.at[core, j, y, b]),
            meanwhile=first,
        )
        both(
            gather_over(place, "x", sems, lambda j: buf.at[core, j, :, a]),
            gather_over(place, "y", sems, lambda j: buf.at[core, :, j, b]),
            meanwhile=second,
        )
        gather("core", lambda j: buf.at[j], third)

    step = gather_over(place, "z", sems, lambda j: qb.at[core, x, y, j])
    ring.pump(1)
    load_acts.wait()
    rows = acts_t[...].astype(F32)
    for c in range(CHIPS):
        block = rows[c * ROWS : (c + 1) * ROWS]
        at_ref[c] = jnp.concatenate([block, jnp.zeros((PAD_ROWS - ROWS, TOK), F32)], axis=0).astype(BF16)
    acts = Exchange(place, "z", sems, lambda j: at_ref.at[j], lambda s, j: ar.at[j])
    done += [step, acts]
    ring.pump(TA - 1)
    ar[z] = at_ref[z]
    step.arrive()
    gather_plane(qb)

    def place_rows(i, carry):
        for c in range(CHIPS):
            qs[pl.ds(pl.multiple_of(c * 992 + i * 32, 32), 32), :] = qb[(*tile_place(i), c)]
        return carry

    lax.fori_loop(0, 31, place_rows, 0)

    tokens = jnp.dot(ga[z], qs[...], preferred_element_type=F32).astype(BF16)
    for c in range(CHIPS):
        term = jnp.dot(at_ref[c], tokens, preferred_element_type=F32)
        pp[:, :, :, c] = term.reshape(CORES, SIDE, SIDE, 8, RANK)
    load_f.wait()
    term = jnp.dot(out_ref[...], qs[...], preferred_element_type=F32)
    term = jnp.concatenate([term, jnp.zeros((PAD_ROWS - ROWS, RANK), F32)], axis=0)
    pp[:, :, :, z] = pp[:, :, :, z] + term.reshape(CORES, SIDE, SIDE, 8, RANK)

    scatter("core", pp, p_core)
    p_one[...] = pp[core] + p_core[0]
    low, high = pl.ds(0, CHIPS // 2), pl.ds(CHIPS // 2, CHIPS // 2)
    both(
        Exchange(place, "x", sems, lambda j: p_one.at[j, :, low], lambda s, j: p_first.at[0, s - 1]),
        Exchange(place, "y", sems, lambda j: p_one.at[:, j, high], lambda s, j: p_first.at[1, s - 1]),
    )
    p_two[0] = (p_one[x, :, low] + p_first[0, 0]) + (p_first[0, 1] + p_first[0, 2])
    p_two[1] = (p_one[:, y, high] + p_first[1, 0]) + (p_first[1, 1] + p_first[1, 2])
    both(
        Exchange(place, "y", sems, lambda j: p_two.at[0, j], lambda s, j: p_second.at[0, s - 1]),
        Exchange(place, "x", sems, lambda j: p_two.at[1, j], lambda s, j: p_second.at[1, s - 1]),
    )
    p_three[low] = (p_two[0, y] + p_second[0, 0]) + (p_second[0, 1] + p_second[0, 2])
    p_three[high] = (p_two[1, x] + p_second[1, 0]) + (p_second[1, 1] + p_second[1, 2])
    scatter("z", p_three, p_z, lambda: ring.pump(TB))
    total = p_three[z]
    for c in range(CHIPS - 1):
        total += p_z[c]
    pe[core, x, y, z] = total
    gather("z", lambda j: pe.at[core, x, y, j], lambda: ring.pump(TC))
    gather_plane(pe)

    rows = pe[...].reshape(CHIPS * PAD_ROWS, RANK)
    gram[...] = exact_dot(rows, rows, (0, 0))
    inverse_factor(gram, linv)
    inverse = linv[...]
    for c in range(CHIPS):
        rows = pe[:, :, :, c].reshape(PAD_ROWS, RANK)
        p_low[c] = close_dot(rows, inverse, (1, 1)).astype(BF16)
    ring.pump(TD)

    u = jnp.zeros((RANK, TOK), F32)
    for c in range(CHIPS):
        u += lax.dot_general(p_low[c], at_ref[c], (((0,), (0,)), ((), ())), preferred_element_type=F32)
    u = u.astype(BF16)
    own_p = p_low[z].T[:, :ROWS]

    def fill(at_core, at_x, first, width):
        at = pl.ds(first, width)
        term = jnp.dot(u, ga[z, :, at], preferred_element_type=F32)
        term += jnp.dot(own_p, out_ref[:, at], preferred_element_type=F32)
        term = term.astype(BF16)
        for k in range(width // 128):
            w[at_core, at_x, k // 2, k % 2] = term[:, k * 128 : (k + 1) * 128].reshape(CHIPS, 16, 128)

    def add_blocks(first, *blocks):
        left = jnp.concatenate([ar[b] for b in blocks], axis=1)

        def one(at_core, at_x, start, width):
            at = pl.ds(start, width)
            right = jnp.concatenate([ga[b, :, at] for b in blocks], axis=0)
            term = jnp.dot(left, right, preferred_element_type=F32)
            acc[:, at] = term if first else acc[:, at] + term

        over_columns(one)

    w[CORES - 1, SIDE - 1, SIDE - 1] = jnp.zeros(w.shape[3:], BF16)
    over_core_columns(1 - core, fill)
    scatter("core", w, w_core, lambda: over_core_columns(core, fill))

    def add_core(i, carry):
        w_one[i] = (w[core, i].astype(F32) + w_core[0, i].astype(F32)).astype(BF16)
        return carry

    lax.fori_loop(0, SIDE, add_core, 0)
    both(
        Exchange(place, "x", sems, lambda j: w_one.at[j, :, 0], lambda s, j: w_first.at[0, s - 1]),
        Exchange(place, "y", sems, lambda j: w_one.at[:, j, 1], lambda s, j: w_first.at[1, s - 1]),
        meanwhile=lambda: (acts.arrive(), ring.arrive(PIECES), add_blocks(True, z, ring.block(0, 1))),
    )

    def sum_of(mine, received):
        return (
            (mine.astype(F32) + received[0].astype(F32))
            + (received[1].astype(F32) + received[2].astype(F32))
        ).astype(BF16)

    w_two[0] = sum_of(w_one[x, :, 0], w_first[0])
    w_two[1] = sum_of(w_one[:, y, 1], w_first[1])
    both(
        Exchange(place, "y", sems, lambda j: w_two.at[0, j], lambda s, j: w_second.at[0, s - 1]),
        Exchange(place, "x", sems, lambda j: w_two.at[1, j], lambda s, j: w_second.at[1, s - 1]),
    )
    total = jnp.stack([sum_of(w_two[0, y], w_second[0]), sum_of(w_two[1, x], w_second[1])])
    for c in range(CHIPS):
        w_three[c] = total[:, c]
    scatter("z", w_three, w_z, lambda: ring.pump(TE))
    mine = w_three[z].astype(F32)
    for c in range(CHIPS - 1):
        mine += w_z[c].astype(F32)
    qa[core, x, y, :, z] = (mine * (1.0 / 32)).astype(BF16)
    gather("z", lambda j: qa.at[core, x, y, :, j], lambda: ring.pump(TF))
    gather_plane(qa)
    ring.arrive(2 * PIECES)
    add_blocks(False, ring.block(1, 1), ring.block(0, 2))
    ring.pump(ring.TURNS - ring.started)

    p_out[...] = close_dot(pe[:, :, :, z].reshape(PAD_ROWS, RANK), inverse, (1, 1))[:ROWS]
    for t in range(9):
        tile = lax.div(z * 31, 4) + t
        block = qa[(*tile_place(lax.div(tile, 2)), lax.rem(tile, 2))].reshape(RANK, 128)
        q_flat[t * 128 : (t + 1) * 128, :] = block.astype(F32).T
    q_out[...] = q_flat[pl.ds(pl.multiple_of(lax.rem(z * 31, 4) * 32, 32), 992), :]

    ring.arrive(3 * PIECES)
    add_blocks(False, ring.block(1, 2), ring.block(0, 3), ring.block(1, 3))
    for step in done:
        step.sent()
    last = ring.block(0, 4)
    left = jnp.concatenate([ar[last], -p_low[z]], axis=1)

    def finish(piece):
        at = columns_of(piece)
        tiles = [qa[t // 32, t // 8 % 4, t // 2 % 4, t % 2].reshape(RANK, 128) for t in tiles_of(piece)]
        right = jnp.concatenate([ga[last, :, at], jnp.concatenate(tiles, axis=1)], axis=0)
        total = acc[:, at] + jnp.dot(left, right, preferred_element_type=F32)
        out_ref[:, at] = (total[:ROWS] + out_ref[:, at].astype(F32)).astype(BF16)

    for i in range(PIECES // 2):
        ring.arrive(3 * PIECES + i + 1)
        finish(i)
        finish(PIECES - 1 - i)
    ring.sent()


def whole(at, g, f, q):
    copies = 128
    vmem = pl.BlockSpec(memory_space=pltpu.VMEM)
    hbm = pl.BlockSpec(memory_space=pltpu.HBM)
    tile = (CHIPS, 16, 128)
    return pl.pallas_call(
        kernel,
        out_shape=(
            jax.ShapeDtypeStruct((ROWS, COLS), BF16),
            jax.ShapeDtypeStruct((ROWS, RANK), F32),
            jax.ShapeDtypeStruct((992, RANK), F32),
        ),
        in_specs=[hbm, hbm, hbm, hbm],
        out_specs=(vmem, vmem, vmem),
        scratch_shapes=[
            pltpu.VMEM((CHIPS, TOK, COLS), BF16),
            pltpu.VMEM((CHIPS * ROWS, TOK), BF16),
            pltpu.VMEM((CHIPS, PAD_ROWS, TOK), BF16),
            pltpu.VMEM((CHIPS, PAD_ROWS, TOK), BF16),
            pltpu.VMEM((PAD_ROWS, COLS), F32),
            pltpu.VMEM((CORES, SIDE, SIDE, CHIPS, 32, RANK), BF16),
            pltpu.VMEM((COLS, RANK), BF16),
            pltpu.VMEM((CORES, SIDE, SIDE, CHIPS, 8, RANK), F32),
            pltpu.VMEM((1, SIDE, SIDE, CHIPS, 8, RANK), F32),
            pltpu.VMEM((SIDE, SIDE, CHIPS, 8, RANK), F32),
            pltpu.VMEM((2, 3, SIDE, CHIPS // 2, 8, RANK), F32),
            pltpu.VMEM((2, SIDE, CHIPS // 2, 8, RANK), F32),
            pltpu.VMEM((2, 3, CHIPS // 2, 8, RANK), F32),
            pltpu.VMEM((CHIPS, 8, RANK), F32),
            pltpu.VMEM((CHIPS - 1, 8, RANK), F32),
            pltpu.VMEM((CORES, SIDE, SIDE, CHIPS, 8, RANK), F32),
            pltpu.VMEM((RANK, RANK), F32),
            pltpu.VMEM((RANK, RANK), F32),
            pltpu.VMEM((CHIPS, PAD_ROWS, RANK), BF16),
            pltpu.VMEM((CORES, SIDE, SIDE, 2, *tile), BF16),
            pltpu.VMEM((1, SIDE, SIDE, 2, *tile), BF16),
            pltpu.VMEM((SIDE, SIDE, 2, *tile), BF16),
            pltpu.VMEM((2, 3, SIDE, *tile), BF16),
            pltpu.VMEM((2, SIDE, *tile), BF16),
            pltpu.VMEM((2, 3, *tile), BF16),
            pltpu.VMEM((CHIPS, 2, 16, 128), BF16),
            pltpu.VMEM((CHIPS - 1, 2, 16, 128), BF16),
            pltpu.VMEM((CORES, SIDE, SIDE, 2, *tile), BF16),
            pltpu.VMEM((9 * 128, RANK), F32),
            pltpu.SemaphoreType.DMA((4,)),
            pltpu.SemaphoreType.DMA((copies,)),
            pltpu.SemaphoreType.DMA((copies,)),
            pltpu.SemaphoreType.DMA((2, Ring.TURNS)),
            pltpu.SemaphoreType.DMA((2, Ring.TURNS)),
        ],
        compiler_params=pltpu.CompilerParams(
            collective_id=0, has_side_effects=True, vmem_limit_bytes=VMEM_MIB * 2**20
        ),
        cost_estimate=pl.CostEstimate(flops=10**10, bytes_accessed=30 * 10**6, transcendentals=0),
    )(at, g, f, q)


def store_kernel(*refs):
    count = (len(refs) - 1) // 2
    copies = [pltpu.make_async_copy(refs[i], refs[count + i], refs[-1].at[i]) for i in range(count)]
    for copy in copies:
        copy.start()
    for copy in copies:
        copy.wait()


def stored(*arrays):
    return pl.pallas_call(
        store_kernel,
        out_shape=tuple(pltpu.HBM(a.shape, a.dtype) for a in arrays),
        in_specs=[pl.BlockSpec(memory_space=pl.ANY)] * len(arrays),
        out_specs=(pl.BlockSpec(memory_space=pltpu.HBM),) * len(arrays),
        scratch_shapes=[pltpu.SemaphoreType.DMA((len(arrays),))],
        compiler_params=pltpu.CompilerParams(vmem_limit_bytes=2**20),
    )(*arrays)


def local(activations, hidden_grad, feedback, q_start):
    here = lambda a: pltpu.with_memory_space_constraint(a, pltpu.HBM)
    return stored(*whole(here(activations.T), here(hidden_grad), here(feedback), here(q_start)))


def solution(mesh):
    in_specs = (
        P(("node", "chip"), None),
        P(("node", "chip"), None),
        P(("node", "chip"), None),
        P("chip", None),
    )
    out_specs = (P(("node", "chip"), None), P("chip", None), P("chip", None))
    return jax.shard_map(local, mesh=mesh, in_specs=in_specs, out_specs=out_specs, check_vma=False)
```
